512 devices in a mesh: pipe: 2 (over z_hi), ctx: 64 (over y, z_lo, core), tp: 4 (over x).
Axes of the slice: x: 4, y: 4, z: 16 (z_hi: 2, z_lo: 8; z = z_hi * 8 + z_lo), core: 2. Of those that a mesh axis runs over, the one named last changes fastest.
Arguments:
- section_output: bfloat16 [2, 8192, 8192], P('pipe', 'ctx', 'tp'), may hold values from -26 to 26
- norm_gain: float32 [2, 8192], P('pipe'), may hold values from 0.1 to 1.9
- kv_weight: bfloat16 [2, 8192, 1024], P('pipe', 'ctx', 'tp'), may hold values from -0.0625 to 0.0625
- queries: bfloat16 [2, 8192, 4096], P('pipe', 'ctx', 'tp'), may hold values from -171 to 171
- rank_block: int32 [128], replicated, may hold values from 0 to 127, each once
Outputs:
- attention: bfloat16 [2, 8192, 4096], P('pipe', 'ctx', 'tp')
- log_total: float32 [2, 8192, 32], P('pipe', 'ctx', 'tp')
The draws below stay inside these ranges and needn't reach their ends.
Inputs may be any that keep to these rules, and one draw needn't show every extreme that they name: `rank_block`: each of 0 to 127 once.
All inputs are finite; a program needn't handle non-finite values.
Results may differ from the reference program's by a relative error of at most 0.017.
The reference program's roundings to bfloat16 on the way (of `received`, `normed`, `keys` and `values`) count: a program that leaves them out, or rounds other values in their place, can miss the bound.
Values may be sent and summed in bfloat16 or wider, within the bound.
No kernel may reach another device: no remote copies, remote signals or barrier semaphores. Data moves between devices by JAX's collectives and lax.ppermute only.
A program may use at most 128 MiB of HBM per device.

```python
import math
import jax
import jax.numpy as jnp
from jax import lax

D = 8192
QH = 32
KVH = 4
HD = 128
TOK_DEV = 128
BLOCKS = 128
SEQ = 8192
SECTIONS = 2
N_CTX = 64


def draw_section_output(key, part):
    first_key, second_key, third_key = jax.random.split(jax.random.fold_in(key, 11), 3)
    shape_all = (SECTIONS, SEQ, D)
    base_vals = jax.random.truncated_normal(first_key, -4.0, 4.0, shape_all, jnp.float32)
    row_scale = jnp.exp(jax.random.uniform(second_key, (SECTIONS, SEQ, 1), jnp.float32, -0.7, 0.7))
    col_scale = jnp.exp(jax.random.uniform(third_key, (1, 1, D), jnp.float32, -1.15, 1.15))
    return (base_vals * row_scale * col_scale).astype(jnp.bfloat16)


def draw_queries(key, part):
    first_key = jax.random.fold_in(jax.random.fold_in(key, 23), 0)
    shape_all = (SECTIONS, SEQ, QH * HD)
    return (jax.random.truncated_normal(first_key, -4.0, 4.0, shape_all, jnp.float32) * 2.5).astype(jnp.bfloat16)


def level_of(own_key, shape, pieces, smallest, largest):
    gain = 1.0
    for axis_at, parts in pieces:
        steps = jax.random.uniform(jax.random.fold_in(jax.random.fold_in(own_key, 6), axis_at), (parts,), jnp.float32, smallest / len(pieces), largest / len(pieces))
        gain = gain * jnp.repeat(jnp.exp(steps), shape[axis_at] // parts).reshape((-1,) + (1,) * (len(shape) - 1 - axis_at))
    return gain


def scatter_about(key, extent, spread, bound, shards=(), kind=jnp.bfloat16):
    values = jax.random.normal(key, extent, jnp.float32) * spread
    if len(shards) > 0:
        values = level_of(key, extent, shards, -0.22, 0.18) * values
    return jnp.clip(values, min=-bound, max=bound).astype(kind)


def setup_inputs(seed: int = 0) -> dict:
    arg_keys = jax.random.split(jax.random.key(seed), 6)
    section_output = draw_section_output(jax.random.fold_in(arg_keys[5], 71), 0)
    norm_gain = jnp.clip(1.0 + 0.18 * jax.random.normal(arg_keys[1], (SECTIONS, D), jnp.float32), 0.1, 1.9)
    kv_weight = scatter_about(arg_keys[2], (SECTIONS, D, 2 * KVH * HD), D ** -0.5, 0.0625, ((0, 2), (1, 64), (2, 4)))
    queries = draw_queries(jax.random.fold_in(arg_keys[5], 71), 0)
    rank_block = jax.random.permutation(arg_keys[4], BLOCKS).astype(jnp.int32)
    return dict(section_output=section_output, norm_gain=norm_gain, kv_weight=kv_weight, queries=queries, rank_block=rank_block)


norm_eps = 1e-05
rope_base = 500000.0
mask_fill = -1e+30

def block_positions(rank_block, ctx_count, half_rows):
    block_ids = rank_block.reshape(ctx_count, 2).astype(jnp.int32)
    within = jnp.arange(half_rows, dtype=jnp.int32)
    return (block_ids[:, :, None] * half_rows + within[None, None, :]).reshape(-1).astype(jnp.int32)

def rotate_keys(raw_keys, positions):
    width = raw_keys.shape[-1]
    half_width = width // 2
    steps_f = jnp.arange(half_width, dtype=jnp.float32)
    inv_freq = jnp.exp(steps_f * (-2.0 / width) * math.log(rope_base))
    angles = positions.astype(jnp.float32)[:, None] * inv_freq[None, :]
    cosine = jnp.cos(angles)
    sine_part = jnp.sin(angles)
    first_half = raw_keys[:, :half_width]
    second_half = raw_keys[:, half_width:]
    return jnp.concatenate([first_half * cosine - second_half * sine_part, second_half * cosine + first_half * sine_part], axis=1)

def attend_head(head_queries, keys, values, positions, score_scale, group_size):
    block_rows = TOK_DEV
    count = SEQ // block_rows
    query_blocks = head_queries.reshape(count, block_rows, group_size, HD)
    pos_blocks = positions.reshape(count, block_rows)
    keys_f = keys.astype(jnp.float32)
    values_f = values.astype(jnp.float32)

    def one_block(operands):
        query_part, query_pos = operands
        logits = jnp.einsum('qgd,kd->gqk', query_part.astype(jnp.float32), keys_f, precision=lax.Precision.HIGHEST) * score_scale
        allowed = positions[None, None, :] <= query_pos[None, :, None]
        logits = jnp.where(allowed, logits, mask_fill)
        row_max = lax.optimization_barrier(jnp.max(logits, axis=-1))
        log_total = row_max + jnp.log(lax.optimization_barrier(jnp.sum(jnp.exp(logits - row_max[..., None]), axis=-1)))
        att_weights = jnp.where(allowed, jnp.exp(logits - log_total[..., None]), 0.0)
        attended = jnp.einsum('gqk,kd->qgd', att_weights, values_f, precision=lax.Precision.HIGHEST).astype(jnp.bfloat16)
        return (attended, jnp.transpose(log_total))
    attended, totals = lax.map(one_block, (query_blocks, pos_blocks))
    return (attended.reshape(SEQ, group_size, HD), totals.reshape(SEQ, group_size))

def reference(section_output, norm_gain, kv_weight, queries, rank_block):
    half_rows = TOK_DEV // 2
    positions = block_positions(rank_block, N_CTX, half_rows)
    group_size = QH // KVH
    score_scale = 1.0 / math.sqrt(HD)
    attn_sections = []
    total_sections = []
    for section_idx in range(SECTIONS):
        received = section_output[(section_idx - 1) % SECTIONS].astype(jnp.float32)
        mean_sq = lax.optimization_barrier(jnp.mean(received * received, axis=-1, keepdims=True))
        normed = (received * lax.rsqrt(mean_sq + norm_eps) * norm_gain[section_idx]).astype(jnp.bfloat16)
        projected = jnp.dot(normed, kv_weight[section_idx], preferred_element_type=jnp.float32)
        head_outs = []
        head_totals = []
        for kv_head in range(KVH):
            base_col = kv_head * 2 * HD
            keys = rotate_keys(projected[:, base_col:base_col + HD], positions).astype(jnp.bfloat16)
            values = projected[:, base_col + HD:base_col + 2 * HD].astype(jnp.bfloat16)
            head_queries = queries[section_idx][:, kv_head * group_size * HD:(kv_head + 1) * group_size * HD].reshape(SEQ, group_size, HD)
            attended, totals = attend_head(head_queries, keys, values, positions, score_scale, group_size)
            head_outs.append(attended.reshape(SEQ, group_size * HD))
            head_totals.append(totals)
        attn_sections.append(jnp.concatenate(head_outs, axis=1))
        total_sections.append(jnp.concatenate(head_totals, axis=1))
    return (jnp.stack(attn_sections), jnp.stack(total_sections))
```

```python
import math

import jax
import jax.numpy as jnp
import numpy as np
from jax import lax
from jax.experimental import pallas as pl
from jax.experimental.pallas import tpu as pltpu
from jax.sharding import Mesh
from jax.sharding import PartitionSpec as P

HD = 128
HEADS = 8
NORM_EPS = 1e-05
ROPE_BASE = 500000.0
NEG = -1e30
SIZES = {"pipe": 2, "y": 4, "zg": 2, "zi": 4, "core": 2, "tp": 4}
AXES = tuple(SIZES)
CTX = ("y", "zg", "zi", "core")
KEY_TILE = 256
VMEM_LIMIT = 56 * 1024 * 1024


def permute(x, axes, move):
    sizes = [SIZES[a] for a in axes]
    pairs = []
    for i in range(int(np.prod(sizes))):
        at = [int(v) for v in np.unravel_index(i, sizes)]
        to = [int(v) % n for v, n in zip(move(*at), sizes)]
        pairs.append((i, int(np.ravel_multi_index(to, sizes))))
    return lax.ppermute(x, axes if len(axes) > 1 else axes[0], pairs)


def spread(unit):
    pair = []
    for u in range(2):
        pair.append(
            permute(
                unit,
                ("pipe", "y", "zg", "zi", "tp"),
                lambda p, y, g, i, t, u=u: (1 - p, t, (i + u) % 2, 3 - (4 * g + i) // 2, y),
            )
        )
    pair = jnp.concatenate(pair, axis=0)
    parts = [pair] + [permute(pair, ("zi",), lambda i, k=k: (i + k,)) for k in (1, 2, 3)]
    own = jnp.stack(parts)
    other = permute(own, ("core",), lambda c: (c + 1,))
    return own, other


def project_kernel(where, acts, sums, gain, own, other, out, weight):
    for from_other, ref in enumerate((own, other)):
        for k in range(4):
            for u in range(2):
                at = where[from_other * 8 + k * 2 + u]
                weight[pl.ds(pl.multiple_of(at * 128, 128), 128), :] = ref[k, u * 128 : (u + 1) * 128, :]
    for y in range(4):
        total = (sums[4 * y] + sums[4 * y + 1]) + (sums[4 * y + 2] + sums[4 * y + 3])
        scale = lax.rsqrt(total * (1.0 / 8192) + NORM_EPS)
        column = jnp.transpose(jnp.broadcast_to(scale[:1], (128, 128)))
        normed = acts[y].astype(jnp.float32) * column[:, :1] * gain[...]
        out[y] = jnp.dot(normed.astype(jnp.bfloat16), weight[...], preferred_element_type=jnp.float32)


def rope_kernel(parts, cos, sin, out):
    total = (parts[0] + parts[1]) + (parts[2] + parts[3])
    raw = total[:, :HD]
    turned = pltpu.roll(raw, HD // 2, 1)
    out[:, :HD] = (raw * cos[...] + turned * sin[...]).astype(jnp.bfloat16)
    out[:, HD:] = total[:, HD:].astype(jnp.bfloat16)


def attend_kernel(meta, q_ref, own, other, out, k_s, v_s, vt_s, q_s, m_s, l_s, acc):
    step = pl.program_id(0)
    rows = HEADS * 64
    factor = math.log2(math.e) / math.sqrt(HD)

    @pl.when(step == 0)
    def _():
        for from_other, ref in enumerate((own, other)):
            for k in range(4):
                for b in range(4):
                    at = pl.multiple_of(meta[from_other * 16 + k * 4 + b] * 64, 64)
                    k_s[pl.ds(at, 64), :] = ref[k, b * 64 : (b + 1) * 64, :HD]
                    v_s[pl.ds(at, 64), :] = ref[k, b * 64 : (b + 1) * 64, HD:]
        for t in range(2048 // KEY_TILE):
            tile = v_s[t * KEY_TILE : (t + 1) * KEY_TILE, :].astype(jnp.float32)
            vt_s[t] = jnp.transpose(tile).astype(jnp.bfloat16)

    for half in range(2):
        for h in range(HEADS):
            q_s[h * 64 : (h + 1) * 64, :] = q_ref[0, half * 64 : (half + 1) * 64, h * HD : (h + 1) * HD]
        before = meta[32 + step * 2 + half]
        has_own = meta[40 + step * 2 + half]
        per_tile = KEY_TILE // 64
        full = before // per_tile
        left = (before - full * per_tile) * 64
        m_s[...] = jnp.full(m_s.shape, NEG, jnp.float32)
        l_s[...] = jnp.zeros(l_s.shape, jnp.float32)
        acc[...] = jnp.zeros(acc.shape, jnp.float32)

        def tile(t, masked):
            keys = k_s[pl.ds(pl.multiple_of(t * KEY_TILE, KEY_TILE), KEY_TILE), :]
            vt = vt_s[t]
            s = lax.dot_general(keys, q_s[...], (((1,), (1,)), ((), ())), preferred_element_type=jnp.float32)
            s = s * factor
            if masked:
                row = lax.broadcasted_iota(jnp.int32, (1, rows), 1)
                limit = left + has_own * ((row & 63) + 1)
                allowed = lax.broadcasted_iota(jnp.int32, (KEY_TILE, rows), 0) < limit
                s = jnp.where(allowed, s, NEG)
            m_old = m_s[:1]
            m_new = jnp.maximum(m_old, jnp.max(s, axis=0, keepdims=True))
            p = jnp.exp2(s - m_new)
            if masked:
                p = jnp.where(allowed, p, 0.0)
            alpha = jnp.exp2(m_old - m_new)
            m_s[:1] = m_new
            l_s[:1] = l_s[:1] * alpha + jnp.sum(p, axis=0, keepdims=True)
            acc[...] = acc[...] * alpha + jnp.dot(vt, p.astype(jnp.bfloat16), preferred_element_type=jnp.float32)

        def whole(t, carry):
            tile(t, False)
            return carry

        lax.fori_loop(0, full, whole, 0)

        @pl.when(left + has_own > 0)
        def _():
            tile(full, True)

        total = l_s[:1]
        some = total > 0.0
        inverse = jnp.where(some, 1.0 / jnp.where(some, total, 1.0), 0.0)
        lse = jnp.where(some, m_s[:1] * math.log(2.0) + jnp.log(jnp.where(some, total, 1.0)), NEG)
        high = lse.astype(jnp.bfloat16).astype(jnp.float32)
        rest = lse - high
        middle = rest.astype(jnp.bfloat16).astype(jnp.float32)
        low = rest - middle
        line = lax.broadcasted_iota(jnp.int32, (128, 128), 0)
        stats = jnp.zeros((64, 128), jnp.float32)
        for pair in range(HEADS // 2):
            cols = slice(pair * 128, (pair + 1) * 128)
            turned = jnp.transpose(acc[:, cols] * inverse[:, cols]).astype(jnp.bfloat16)
            out[0, half * 64 : (half + 1) * 64, (2 * pair) * HD : (2 * pair + 1) * HD] = turned[:64]
            out[0, half * 64 : (half + 1) * 64, (2 * pair + 1) * HD : (2 * pair + 2) * HD] = turned[64:]
            pieces = jnp.where(
                line == 0,
                high[:, cols],
                jnp.where(line == 8, middle[:, cols], jnp.where(line == 16, low[:, cols], 0.0)),
            )
            pieces = jnp.transpose(pieces)
            for odd in range(2):
                head = 2 * pair + odd
                part = pieces[odd * 64 : (odd + 1) * 64]
                stats = stats + (pltpu.roll(part, head, 1) if head else part)
        out[0, half * 64 : (half + 1) * 64, HEADS * HD :] = stats.astype(jnp.bfloat16)


def merge_kernel(parts, out, log_total):
    logs = []
    for i in range(4):
        pieces = parts[i, :, HEADS * HD :].astype(jnp.float32)
        logs.append((pieces + pltpu.roll(pieces, 120, 1)) + pltpu.roll(pieces, 112, 1))
    top = jnp.maximum(jnp.maximum(logs[0], logs[1]), jnp.maximum(logs[2], logs[3]))
    weights = [jnp.exp(v - top) for v in logs]
    total = (weights[0] + weights[1]) + (weights[2] + weights[3])
    log_total[...] = (top + jnp.log(total))[:, :HEADS]
    weights = [w / total for w in weights]
    for h in range(HEADS):
        cols = slice(h * HD, (h + 1) * HD)
        acc = weights[0][:, h : h + 1] * parts[0, :, cols].astype(jnp.float32)
        for i in range(1, 4):
            acc = acc + weights[i][:, h : h + 1] * parts[i, :, cols].astype(jnp.float32)
        out[:, cols] = acc.astype(jnp.bfloat16)


def params(**kw):
    return pltpu.CompilerParams(vmem_limit_bytes=VMEM_LIMIT, **kw)


SMEM = pl.BlockSpec(memory_space=pltpu.SMEM)
VMEM = pl.BlockSpec(memory_space=pltpu.VMEM)


def body(section_output, norm_gain, kv_weight, queries, rank_block):
    y, g, i = lax.axis_index("y"), lax.axis_index("zg"), lax.axis_index("zi")
    c, t = lax.axis_index("core"), lax.axis_index("tp")
    z = g * 4 + i
    acts = section_output[0]

    w_own, w_other = spread(kv_weight[0])
    gain = lax.dynamic_slice(norm_gain, (0, t * 2048), (1, 2048))
    gain = permute(gain, ("pipe", "zg", "zi"), lambda p, a, b: (1 - p, 1 - a, 3 - b))

    square = jnp.sum(jnp.square(acts.astype(jnp.float32)), axis=1)
    square = jnp.broadcast_to(square[None, None, :], (16, 8, 128))
    sums = lax.all_to_all(square, ("y", "tp"), 0, 0, tiled=True)
    acts_y = lax.all_gather(acts, "y", axis=0)
    q_y = lax.all_gather(queries[0], "y", axis=0)

    k_index = jnp.arange(4, dtype=jnp.int32)[:, None]
    u_index = jnp.arange(2, dtype=jnp.int32)[None, :]
    from_z = (2 * (3 - (i - k_index) % 4) + (u_index ^ g)).reshape(-1)
    places = jnp.concatenate([2 * from_z + c, 2 * from_z + 1 - c])

    partial = pl.pallas_call(
        project_kernel,
        out_shape=jax.ShapeDtypeStruct((4, 128, 256), jnp.float32),
        in_specs=[SMEM] + [VMEM] * 5,
        out_specs=VMEM,
        scratch_shapes=[pltpu.VMEM((2048, 256), jnp.bfloat16)],
        compiler_params=params(),
        name="project",
    )(places, acts_y, sums, gain, w_own, w_other)
    partial = lax.all_to_all(partial, "tp", 0, 0, tiled=True)

    half_row = jnp.arange(128, dtype=jnp.int32)
    rank = 16 * t + 2 * z + c
    blocks = lax.dynamic_slice(rank_block, (2 * rank,), (2,))
    pos = jnp.where(half_row < 64, blocks[0], blocks[1]) * 64 + (half_row & 63)
    inv_freq = jnp.exp(jnp.arange(HD // 2, dtype=jnp.float32) * (-2.0 / HD) * math.log(ROPE_BASE))
    angles = pos.astype(jnp.float32)[:, None] * inv_freq[None, :]
    cos, sin = jnp.cos(angles), jnp.sin(angles)
    cos = jnp.concatenate([cos, cos], axis=1)
    sin = jnp.concatenate([-sin, sin], axis=1)
    unit = pl.pallas_call(
        rope_kernel,
        out_shape=jax.ShapeDtypeStruct((128, 256), jnp.bfloat16),
        in_specs=[VMEM] * 3,
        out_specs=VMEM,
        compiler_params=params(),
        name="rope",
    )(partial, cos, sin)
    kv_own, kv_other = spread(unit)

    ranks = 16 * y + places
    ids = rank_block[(2 * ranks[:, None] + jnp.arange(2, dtype=jnp.int32)[None, :]).reshape(-1)]
    order = jnp.sum((ids[None, :] < ids[:, None]).astype(jnp.int32), axis=1)
    q_ranks = 16 * jnp.arange(4, dtype=jnp.int32) + 2 * z + c
    q_ids = rank_block[(2 * q_ranks[:, None] + jnp.arange(2, dtype=jnp.int32)[None, :]).reshape(-1)]
    before = jnp.sum((ids[None, :] < q_ids[:, None]).astype(jnp.int32), axis=1)
    has_own = jnp.sum((ids[None, :] == q_ids[:, None]).astype(jnp.int32), axis=1)
    meta = jnp.concatenate([order, before, has_own])

    rows = HEADS * 64
    width = HEADS * HD + 128
    shares = pl.pallas_call(
        attend_kernel,
        out_shape=jax.ShapeDtypeStruct((4, 128, width), jnp.bfloat16),
        grid_spec=pltpu.PrefetchScalarGridSpec(
            num_scalar_prefetch=1,
            grid=(4,),
            in_specs=[
                pl.BlockSpec((1, 128, HEADS * HD), lambda s, _: (s, 0, 0)),
                pl.BlockSpec((4, 256, 256), lambda s, _: (0, 0, 0)),
                pl.BlockSpec((4, 256, 256), lambda s, _: (0, 0, 0)),
            ],
            out_specs=pl.BlockSpec((1, 128, width), lambda s, _: (s, 0, 0)),
            scratch_shapes=[
                pltpu.VMEM((2048, HD), jnp.bfloat16),
                pltpu.VMEM((2048, HD), jnp.bfloat16),
                pltpu.VMEM((2048 // KEY_TILE, HD, KEY_TILE), jnp.bfloat16),
                pltpu.VMEM((rows, HD), jnp.bfloat16),
                pltpu.VMEM((8, rows), jnp.float32),
                pltpu.VMEM((8, rows), jnp.float32),
                pltpu.VMEM((HD, rows), jnp.float32),
            ],
        ),
        compiler_params=params(),
        name="attend",
    )(meta, q_y, kv_own, kv_other)
    shares = lax.all_to_all(shares, "y", 0, 0, tiled=True)
    attention, log_total = pl.pallas_call(
        merge_kernel,
        out_shape=(
            jax.ShapeDtypeStruct((128, HEADS * HD), jnp.bfloat16),
            jax.ShapeDtypeStruct((128, HEADS), jnp.float32),
        ),
        in_specs=[VMEM],
        out_specs=(VMEM, VMEM),
        compiler_params=params(),
        name="merge",
    )(shares)
    return attention[None], log_total[None]


def solution(mesh):
    fine = Mesh(mesh.devices.reshape(tuple(SIZES.values())), AXES)
    split = P("pipe", CTX, "tp")
    return jax.shard_map(
        body,
        mesh=fine,
        in_specs=(split, P("pipe", None), split, split, P()),
        out_specs=(split, split),
        check_vma=False,
    )
```

```python
import functools
import math

import jax
import jax.numpy as jnp
import numpy as np
from jax import lax
from jax.experimental import pallas as pl
from jax.experimental.pallas import tpu as pltpu
from jax.sharding import Mesh
from jax.sharding import PartitionSpec as P

HD = 128
HEADS = 8
NORM_EPS = 1e-05
ROPE_BASE = 500000.0
NEG = -1e30
SIZES = {"pipe": 2, "y": 4, "zg": 2, "zi": 4, "core": 2, "tp": 4}
AXES = tuple(SIZES)
CTX = ("y", "zg", "zi", "core")
KEY_TILE = 512
VMEM_LIMIT = 56 * 1024 * 1024


def permute(x, axes, move):
    sizes = [SIZES[a] for a in axes]
    pairs = []
    for i in range(int(np.prod(sizes))):
        at = [int(v) for v in np.unravel_index(i, sizes)]
        to = [int(v) % n for v, n in zip(move(*at), sizes)]
        pairs.append((i, int(np.ravel_multi_index(to, sizes))))
    return lax.ppermute(x, axes if len(axes) > 1 else axes[0], pairs)


TAKES = (
    (3, 5, 7, 0, 6, 1, 2, 4),
    (2, 4, 6, 1, 7, 0, 3, 5),
)


def stack_kernel(*refs):
    out = refs[-1]
    for k in range(4):
        out[k] = refs[k][...]


def join_kernel(*refs):
    out = refs[-1]
    out[:128] = refs[0][...]
    out[128:] = refs[1][...]


def spread(unit, early, late):
    pair = []
    for takes in TAKES:
        pair.append(
            permute(
                unit,
                ("pipe", "y", "zg", "zi", "tp"),
                lambda p, y, g, i, t, takes=takes: (
                    1 - p,
                    t,
                    takes.index(4 * g + i) // 4,
                    takes.index(4 * g + i) % 4,
                    y,
                ),
            )
        )
    pair = pl.pallas_call(
        join_kernel,
        out_shape=pltpu.VMEM((256, 256), jnp.bfloat16),
        in_specs=[VMEM] * (2 + len(early)),
        out_specs=VMEM,
        compiler_params=params(),
        name="join",
    )(*near(*pair, *early))
    late = late(pair)
    parts = [pair] + [permute(pair, ("zi",), lambda i, k=k: (i + k,)) for k in (1, 2, 3)]
    own = pl.pallas_call(
        stack_kernel,
        out_shape=pltpu.VMEM((4, 256, 256), jnp.bfloat16),
        in_specs=[VMEM] * (4 + len(late)),
        out_specs=VMEM,
        compiler_params=params(),
        name="stack",
    )(*near(*parts, *late))
    other = permute(own, ("core",), lambda c: (c + 1,))
    return own, other, late


def squares_kernel(acts, after, out):
    del after
    rows = acts[...].astype(jnp.float32)
    total = jnp.sum(rows * rows, axis=1, keepdims=True)
    line = jnp.transpose(jnp.broadcast_to(total, (128, 128)))[:8]
    for i in range(16):
        out[i] = line


def project_kernel(where, acts0, acts1, acts2, acts3, sums, gain, own, other, out, weight):
    for from_other, ref in enumerate((own, other)):
        for k in range(4):
            for u in range(2):
                at = where[from_other * 8 + k * 2 + u]
                weight[pl.ds(pl.multiple_of(at * 128, 128), 128), :] = ref[k, u * 128 : (u + 1) * 128, :]
    for k, acts in enumerate((acts0, acts1, acts2, acts3)):
        y = where[16 + k]
        total = (sums[4 * y] + sums[4 * y + 1]) + (sums[4 * y + 2] + sums[4 * y + 3])
        scale = lax.rsqrt(total * (1.0 / 8192) + NORM_EPS)
        column = jnp.transpose(jnp.broadcast_to(scale[:1], (128, 128)))
        normed = acts[...].astype(jnp.float32) * column[:, :1] * gain[...]
        out[y] = jnp.dot(normed.astype(jnp.bfloat16), weight[...], preferred_element_type=jnp.float32)


def rope_kernel(meta, parts, cos, sin, out):
    del meta
    total = (parts[0] + parts[1]) + (parts[2] + parts[3])
    raw = total[:, :HD]
    turned = pltpu.roll(raw, HD // 2, 1)
    out[:, :HD] = (raw * cos[...] + turned * sin[...]).astype(jnp.bfloat16)
    out[:, HD:] = total[:, HD:].astype(jnp.bfloat16)


def sort_blocks(meta, own, other, k_s, v_s):
    v_s[:, HD:] = jnp.ones((2048, HD), jnp.bfloat16)
    for from_other, ref in enumerate((own, other)):
        for k in range(4):
            for b in range(4):
                at = pl.multiple_of(meta[from_other * 16 + k * 4 + b] * 64, 64)
                k_s[pl.ds(at, 64), :] = ref[k, b * 64 : (b + 1) * 64, :HD]
                v_s[pl.ds(at, 64), :HD] = ref[k, b * 64 : (b + 1) * 64, HD:]


def attend(slot, meta, q_ref, k_s, v_s, out, s_buf, q_s, top, acc):
    rows = HEADS * 64
    factor = math.log2(math.e) / math.sqrt(HD)
    per_tile = KEY_TILE // 64
    lane = lax.broadcasted_iota(jnp.int32, (64, 128), 1)
    for half in range(2):
        here = slice(half * 64, (half + 1) * 64)
        before = meta[32 + slot * 2 + half]
        has_own = meta[40 + slot * 2 + half]
        full = before // per_tile
        left = (before - full * per_tile) * 64
        extra = jnp.minimum(left + has_own, 1)

        @pl.when(before + has_own == 0)
        def _():
            out[here, : HEADS * HD] = jnp.zeros((64, HEADS * HD), jnp.bfloat16)
            out[here, HEADS * HD :] = jnp.where(lane < HEADS, NEG, 0.0).astype(jnp.bfloat16)

        @pl.when(before + has_own > 0)
        def _():
            for h in range(HEADS):
                q_s[h * 64 : (h + 1) * 64, :] = q_ref[here, h * HD : (h + 1) * HD]
            top[...] = jnp.full(top.shape, NEG, jnp.float32)
            acc[...] = jnp.zeros(acc.shape, jnp.float32)

            def scores(t, masked):
                keys = k_s[pl.ds(pl.multiple_of(t * KEY_TILE, KEY_TILE), KEY_TILE), :]
                s = lax.dot_general(
                    q_s[...], keys, (((1,), (1,)), ((), ())), preferred_element_type=jnp.float32
                )
                if masked:
                    row = lax.broadcasted_iota(jnp.int32, (rows, KEY_TILE), 0) & 63
                    limit = left + has_own * (row + 1)
                    s = jnp.where(lax.broadcasted_iota(jnp.int32, (rows, KEY_TILE), 1) < limit, s, NEG)
                s_buf[t] = s
                best = top[...]
                for j in range(KEY_TILE // 128):
                    best = jnp.maximum(best, s[:, j * 128 : (j + 1) * 128])
                top[...] = best

            def whole(t, carry):
                scores(t, False)
                return carry

            lax.fori_loop(0, full, whole, 0)

            @pl.when(extra > 0)
            def _():
                scores(full, True)

            best = jnp.max(top[...], axis=1, keepdims=True) * factor
            top[...] = jnp.broadcast_to(best, top.shape)

            def gather(t, carry):
                best = top[...]
                p = jnp.concatenate(
                    [
                        jnp.exp2(s_buf[t, :, j * 128 : (j + 1) * 128] * factor - best).astype(jnp.bfloat16)
                        for j in range(KEY_TILE // 128)
                    ],
                    axis=1,
                )
                values = v_s[pl.ds(pl.multiple_of(t * KEY_TILE, KEY_TILE), KEY_TILE), :]
                acc[...] += jnp.dot(p, values, preferred_element_type=jnp.float32)
                return carry

            lax.fori_loop(0, full + extra, gather, 0)

            stats = jnp.zeros((64, 128), jnp.float32)
            for h in range(HEADS):
                part = slice(h * 64, (h + 1) * 64)
                total = acc[part, HD:]
                out[here, h * HD : (h + 1) * HD] = (acc[part, :HD] / total).astype(jnp.bfloat16)
                lse = top[part] * math.log(2.0) + jnp.log(total)
                high = lse.astype(jnp.bfloat16).astype(jnp.float32)
                rest = lse - high
                middle = rest.astype(jnp.bfloat16).astype(jnp.float32)
                stats = jnp.where(lane == h, high, stats)
                stats = jnp.where(lane == 8 + h, middle, stats)
                stats = jnp.where(lane == 16 + h, rest - middle, stats)
            out[here, HEADS * HD :] = stats.astype(jnp.bfloat16)


def attend_first_kernel(slot, meta, q_ref, own, other, out, k_s, v_s, *scratch):
    sort_blocks(meta, own, other, k_s, v_s)
    attend(slot, meta, q_ref, k_s, v_s, out, *scratch)


def attend_next_kernel(slot, meta, q_ref, k_s, v_s, out, *scratch):
    attend(slot, meta, q_ref, k_s, v_s, out, *scratch)


def merge_kernel(first, second, third, fourth, out, log_total):
    parts = (first, second, third, fourth)
    logs = []
    for part in parts:
        pieces = part[:, HEADS * HD :].astype(jnp.float32)
        logs.append((pieces + pltpu.roll(pieces, 120, 1)) + pltpu.roll(pieces, 112, 1))
    top = jnp.maximum(jnp.maximum(logs[0], logs[1]), jnp.maximum(logs[2], logs[3]))
    weights = [jnp.exp(v - top) for v in logs]
    total = (weights[0] + weights[1]) + (weights[2] + weights[3])
    log_total[...] = jnp.transpose(top + jnp.log(total))[:HEADS]
    weights = [w / total for w in weights]
    for h in range(HEADS):
        cols = slice(h * HD, (h + 1) * HD)
        acc = weights[0][:, h : h + 1] * parts[0][:, cols].astype(jnp.float32)
        for i in range(1, 4):
            acc = acc + weights[i][:, h : h + 1] * parts[i][:, cols].astype(jnp.float32)
        out[:, cols] = acc.astype(jnp.bfloat16)


def near(*arrays):
    return [pltpu.with_memory_space_constraint(x, pltpu.VMEM) for x in arrays]


def params(**kw):
    return pltpu.CompilerParams(vmem_limit_bytes=VMEM_LIMIT, **kw)


SMEM = pl.BlockSpec(memory_space=pltpu.SMEM)
VMEM = pl.BlockSpec(memory_space=pltpu.VMEM)


def body(section_output, norm_gain, kv_weight, queries, rank_block):
    y, g, i = lax.axis_index("y"), lax.axis_index("zg"), lax.axis_index("zi")
    c, t = lax.axis_index("core"), lax.axis_index("tp")
    z = g * 4 + i
    acts = section_output[0]
    k_index = jnp.arange(4, dtype=jnp.int32)

    acts_y = [acts] + [permute(acts, ("y",), lambda r, k=k: (r + k,)) for k in (1, 2, 3)]

    def square_sums(after):
        squares = pl.pallas_call(
            squares_kernel,
            out_shape=pltpu.VMEM((16, 8, 128), jnp.float32),
            in_specs=[VMEM] * 2,
            out_specs=VMEM,
            compiler_params=params(),
            name="squares",
        )(acts, *near(after))
        return (lax.all_to_all(squares, ("y", "tp"), 0, 0, tiled=True), *acts_y[1:])

    gain = lax.dynamic_slice(norm_gain, (0, t * 2048), (1, 2048))
    gain = permute(gain, ("pipe", "zg", "zi"), lambda p, a, b: (1 - p, 1 - a, 3 - b))
    w_own, w_other, (sums, *_) = spread(kv_weight[0], (gain,), square_sums)

    at = 4 * g + (i - k_index) % 4
    from_z = jnp.stack([jnp.array(takes, jnp.int32)[at] for takes in TAKES], axis=1).reshape(-1)
    places = jnp.concatenate([2 * from_z + c, 2 * from_z + 1 - c])
    rows_of = (y - k_index) % 4

    partial = pl.pallas_call(
        project_kernel,
        out_shape=pltpu.VMEM((4, 128, 256), jnp.float32),
        in_specs=[SMEM] + [VMEM] * 8,
        out_specs=VMEM,
        scratch_shapes=[pltpu.VMEM((2048, 256), jnp.bfloat16)],
        compiler_params=params(),
        name="project",
    )(jnp.concatenate([places, rows_of]), *near(*acts_y, sums, gain, w_own, w_other))
    parts = lax.all_to_all(partial, "tp", 0, 0, tiled=True)

    halves = jnp.arange(2, dtype=jnp.int32)[None, :]
    ids = rank_block[(2 * (16 * y + places)[:, None] + halves).reshape(-1)]
    order = jnp.sum((ids[None, :] < ids[:, None]).astype(jnp.int32), axis=1)
    q_ids = rank_block[(2 * (16 * rows_of + 2 * z + c)[:, None] + halves).reshape(-1)]
    before = jnp.sum((ids[None, :] < q_ids[:, None]).astype(jnp.int32), axis=1)
    has_own = jnp.sum((ids[None, :] == q_ids[:, None]).astype(jnp.int32), axis=1)
    meta = jnp.concatenate([order, before, has_own])

    half_row = jnp.arange(128, dtype=jnp.int32)
    blocks = lax.dynamic_slice(rank_block, (2 * (16 * t + 2 * z + c),), (2,))
    pos = jnp.where(half_row < 64, blocks[0], blocks[1]) * 64 + (half_row & 63)
    inv_freq = jnp.exp(jnp.arange(HD // 2, dtype=jnp.float32) * (-2.0 / HD) * math.log(ROPE_BASE))
    angles = pos.astype(jnp.float32)[:, None] * inv_freq[None, :]
    cos, sin = jnp.cos(angles), jnp.sin(angles)
    cos = jnp.concatenate([cos, cos], axis=1)
    sin = jnp.concatenate([-sin, sin], axis=1)
    unit = pl.pallas_call(
        rope_kernel,
        out_shape=pltpu.VMEM((128, 256), jnp.bfloat16),
        in_specs=[SMEM] + [VMEM] * 3,
        out_specs=VMEM,
        compiler_params=params(),
        name="rope",
    )(meta, *near(parts, cos, sin))
    own_q = lax.optimization_barrier((queries[0], w_other))[0]
    q_y = [own_q] + [permute(own_q, ("y",), lambda r, k=k: (r + k,)) for k in (1, 2, 3)]
    kv_own, kv_other, _ = spread(unit, q_y[1:], lambda pair: ())

    rows = HEADS * 64
    width = HEADS * HD + 128
    share = pltpu.VMEM((128, width), jnp.bfloat16)
    tables = (pltpu.VMEM((2048, HD), jnp.bfloat16), pltpu.VMEM((2048, 2 * HD), jnp.bfloat16))
    scratch = [
        pltpu.VMEM((2048 // KEY_TILE, rows, KEY_TILE), jnp.float32),
        pltpu.VMEM((rows, HD), jnp.bfloat16),
        pltpu.VMEM((rows, 128), jnp.float32),
        pltpu.VMEM((rows, 2 * HD), jnp.float32),
    ]
    shares = []
    for k in (2, 1, 3, 0):
        if k == 2:
            mine, *sorted_kv = pl.pallas_call(
                functools.partial(attend_first_kernel, k),
                out_shape=(share, *tables),
                in_specs=[SMEM] + [VMEM] * 3,
                out_specs=(VMEM,) * 3,
                scratch_shapes=scratch,
                compiler_params=params(),
                name=f"attend{k}",
            )(meta, *near(q_y[k], kv_own, kv_other))
        else:
            mine = pl.pallas_call(
                functools.partial(attend_next_kernel, k),
                out_shape=share,
                in_specs=[SMEM] + [VMEM] * 3,
                out_specs=VMEM,
                scratch_shapes=scratch,
                compiler_params=params(),
                name=f"attend{k}",
            )(meta, *near(q_y[k], *sorted_kv))
        shares.append(permute(mine, ("y",), lambda r, k=k: (r - k,)) if k else mine)
    attention, log_total = pl.pallas_call(
        merge_kernel,
        out_shape=(
            jax.ShapeDtypeStruct((128, HEADS * HD), jnp.bfloat16),
            jax.ShapeDtypeStruct((HEADS, 128), jnp.float32),
        ),
        in_specs=[VMEM] * 4,
        out_specs=(VMEM, VMEM),
        compiler_params=params(),
        name="merge",
    )(*near(*shares))
    return attention[None], jnp.transpose(log_total)[None]


def solution(mesh):
    fine = Mesh(mesh.devices.reshape(tuple(SIZES.values())), AXES)
    split = P("pipe", CTX, "tp")
    return jax.shard_map(
        body,
        mesh=fine,
        in_specs=(split, P("pipe", None), split, split, P()),
        out_specs=(split, split),
        check_vma=False,
    )
```
